512 devices in a mesh: outer: 16 (over y, x_lo), inner: 32 (over z, x_hi, core).
Axes of the slice: x: 4 (x_hi: 2, x_lo: 2; x = x_hi * 2 + x_lo), y: 8, z: 8, core: 2. Of those that a mesh axis runs over, the one named last changes fastest.
Arguments:
- queries: bfloat16 [131072, 2048], P(('outer', 'inner')), may hold values from -4 to 4
- key_rows: bfloat16 [131072, 128], P(('outer', 'inner')), may hold values from -4 to 4
- value_rows: bfloat16 [131072, 128], P(('outer', 'inner')), may hold values from -6 to 6
- out_grad: bfloat16 [131072, 2048], P(('outer', 'inner')), may hold values from -96 to 96
- outputs: bfloat16 [131072, 2048], P(('outer', 'inner')), may hold values from -1.75 to 1.75
- log_sum: float32 [16, 131072], P(None, ('outer', 'inner')), may hold values from 6 to 7.5
- span_table: int32 [512, 2], replicated, may hold values from 0 to 1023, as said below
Outputs:
- query_grad: bfloat16 [131072, 2048], P(('outer', 'inner'))
- key_grad: float32 [131072, 128], P(('outer', 'inner'))
- value_grad: float32 [131072, 128], P(('outer', 'inner'))
The draws below stay inside these ranges and needn't reach their ends.
Inputs may be any that keep to these rules, and one draw needn't show every extreme that they name: `span_table`: row e holds spans p and 1023 - p, where p over the rows is a permutation of 0 to 511.
All inputs are finite; a program needn't handle non-finite values.
Results may differ from the reference program's by a relative error of at most 0.0075.
Values may be sent and summed in bfloat16 or wider, within the bound.
No kernel may reach another device: no remote copies, remote signals or barrier semaphores. Data moves between devices by JAX's collectives and lax.ppermute only.
A program may use at most 64 MiB of HBM per device.

```python
import math
import jax
import jax.numpy as jnp
from jax import lax

HD = 128
GROUP = 16
SPAN = 128
OUT_STEPS = 2
IN_STEPS = 2
SPANS = 1024
SEQ = 131072
N_OUTER = 16
N_INNER = 32


def draw_span_table(key, part):
    key = jax.random.fold_in(key, 11)
    leading = jax.random.permutation(key, SPANS // 2).astype(jnp.int32)
    return jnp.stack([leading, SPANS - 1 - leading], axis=1).astype(jnp.int32)


def shard_levels(stream_key, shape, shards, low, largest):
    def one(dim, shards_of):
        steps = jax.random.uniform(jax.random.fold_in(jax.random.fold_in(stream_key, 6), dim), (shards_of,), jnp.float32, low / len(shards), largest / len(shards))
        return jnp.repeat(jnp.exp(steps), shape[dim] // shards_of).reshape((-1,) + (1,) * (len(shape) - dim - 1))

    factor_of = one(*shards[0])
    for cut in shards[1:]:
        factor_of = factor_of * one(*cut)
    return factor_of


def normal_values(key, extent, deviation, most, pieces=(), kind=jnp.bfloat16):
    factor_of = shard_levels(key, extent, pieces, -0.22, 0.18) if pieces else 1.0
    result = jax.random.normal(key, extent, jnp.float32) * deviation * factor_of
    return jnp.minimum(jnp.maximum(result, -most), most).astype(kind)


def setup_inputs(seed: int = 0) -> dict:
    splits = jax.random.split(jax.random.key(seed), 8)
    return {
        "queries": normal_values(splits[0], (SEQ, GROUP * HD), 1.0, 4.0, ((0, 512),)),
        "key_rows": normal_values(splits[1], (SEQ, HD), 1.0, 4.0, ((0, 512),)),
        "value_rows": normal_values(splits[2], (SEQ, HD), 1.0, 6.0, ((0, 512),)),
        "out_grad": normal_values(splits[3], (SEQ, GROUP * HD), 16.0, 96.0, ((0, 512),)),
        "outputs": normal_values(splits[4], (SEQ, GROUP * HD), 0.3, 1.75, ((0, 512),)),
        "log_sum": jnp.clip(6.0 + 1.5 * jax.random.uniform(splits[5], (GROUP, SEQ), jnp.float32) ** shard_levels(splits[5], (GROUP, SEQ), ((1, 512),), -0.2, 0.2), 6.0, 7.5),
        "span_table": draw_span_table(jax.random.fold_in(splits[7], 71), 0),
    }


def rounded(values):
    return lax.optimization_barrier(values.astype(jnp.bfloat16)).astype(jnp.float32)

def block_grads(query_block, key_block, value_block, grad_block, log_block, row_dot, query_pos, key_pos, factor):
    query_wide = query_block.astype(jnp.float32)
    key_wide = key_block.astype(jnp.float32)
    value_wide = value_block.astype(jnp.float32)
    grad_wide = grad_block.astype(jnp.float32)
    scores = jnp.einsum('qgd,kd->gqk', query_wide, key_wide) * factor
    visible = key_pos[None, None, :] <= query_pos[None, :, None]
    weights = jnp.where(visible, jnp.exp(scores - log_block[:, :, None]), 0.0)
    dweights = jnp.einsum('qgd,kd->gqk', grad_wide, value_wide)
    dscores = weights * (dweights - row_dot[:, :, None])
    weights_low = rounded(weights)
    dscores_low = rounded(dscores)
    value_part = jnp.einsum('gqk,qgd->kd', weights_low, grad_wide)
    key_part = jnp.einsum('gqk,qgd->kd', dscores_low, query_wide)
    query_part = jnp.einsum('gqk,kd->qgd', dscores_low, key_wide)
    return (query_part, key_part, value_part)

def reference(queries, key_rows, value_rows, out_grad, outputs, log_sum, span_table):
    block_count = N_OUTER * N_INNER
    row_count = 2 * SPAN
    factor = 1.0 / math.sqrt(HD)
    query_all = queries.reshape(block_count, row_count, GROUP, HD)
    grad_all = out_grad.reshape(block_count, row_count, GROUP, HD)
    output_all = outputs.reshape(block_count, row_count, GROUP, HD)
    key_all = key_rows.reshape(block_count, row_count, HD)
    value_all = value_rows.reshape(block_count, row_count, HD)
    log_all = log_sum.reshape(GROUP, block_count, row_count).transpose(1, 0, 2)
    offsets = jnp.arange(SPAN, dtype=jnp.int32)
    positions = (span_table[:, :, None] * SPAN + offsets[None, None, :]).reshape(block_count, row_count)

    def per_block(block_index):
        outer_index = block_index // N_INNER
        inner_index = block_index % N_INNER
        query_block = query_all[block_index]
        grad_block = grad_all[block_index]
        row_dot = lax.optimization_barrier(jnp.sum(grad_block.astype(jnp.float32) * output_all[block_index].astype(jnp.float32), axis=-1)).T
        log_block = log_all[block_index]
        query_pos = positions[block_index]
        query_total = jnp.zeros((row_count, GROUP, HD), jnp.float32)
        key_parts = []
        value_parts = []
        for a in range(OUT_STEPS):
            for b in range(IN_STEPS):
                source = ((outer_index - a) % N_OUTER * N_INNER + (inner_index - b) % N_INNER).astype(jnp.int32)
                query_part, key_part, value_part = block_grads(query_block, key_all[source], value_all[source], grad_block, log_block, row_dot, query_pos, positions[source], factor)
                query_total = query_total + query_part
                key_parts.append(key_part)
                value_parts.append(value_part)
        query_out = (query_total * factor).astype(jnp.bfloat16).reshape(row_count, GROUP * HD)
        return (query_out, jnp.stack(key_parts), jnp.stack(value_parts))
    query_out, key_stack, value_stack = lax.map(per_block, jnp.arange(block_count, dtype=jnp.int32))
    key_stack = key_stack.reshape(N_OUTER, N_INNER, OUT_STEPS * IN_STEPS, row_count, HD)
    value_stack = value_stack.reshape(N_OUTER, N_INNER, OUT_STEPS * IN_STEPS, row_count, HD)
    key_total = jnp.zeros((N_OUTER, N_INNER, row_count, HD), jnp.float32)
    value_total = jnp.zeros((N_OUTER, N_INNER, row_count, HD), jnp.float32)
    for a in range(OUT_STEPS):
        for b in range(IN_STEPS):
            step = a * IN_STEPS + b
            key_total = key_total + jnp.roll(key_stack[:, :, step], (-a, -b), axis=(0, 1))
            value_total = value_total + jnp.roll(value_stack[:, :, step], (-a, -b), axis=(0, 1))
    key_grad = (key_total * factor).reshape(SEQ, HD)
    value_grad = value_total.reshape(SEQ, HD)
    return (query_out.reshape(SEQ, GROUP * HD), key_grad, value_grad)
```

```python
import functools
import math

import jax
import jax.numpy as jnp
from jax import lax
from jax.experimental import pallas as pl
from jax.experimental.pallas import tpu as pltpu
from jax.sharding import PartitionSpec as P

F32 = jnp.float32
BF16 = jnp.bfloat16
HEADS = 16
HD = 128
SPAN = 128
WIDE = HEADS * HD
FACTOR = 1.0 / math.sqrt(HD)
LOG2E = math.log2(math.e)


def dot(a, b, contract):
    return lax.dot_general(a, b, ((contract[:1], contract[1:]), ((), ())), preferred_element_type=F32)


def heads_of(ref, rows):
    return [ref[rows, h * HD : (h + 1) * HD] for h in range(HEADS)]


def sub_block(key, value, queries, grads, log_two, row_dot, mask=None):
    probs, dscores = [], []
    for m in range(0, HEADS, 2):
        pair = jnp.concatenate(queries[m : m + 2], 0)
        grad = jnp.concatenate(grads[m : m + 2], 0)
        lanes = lambda x: jnp.concatenate([x[m : m + 1], x[m + 1 : m + 2]], 1)
        scores = dot(key, pair, (1, 1))
        weights = jnp.exp2(scores * (FACTOR * LOG2E) - lanes(log_two))
        if mask is not None:
            weights = jnp.where(mask, weights, 0.0)
        dweights = dot(value, grad, (1, 1))
        probs.append(weights.astype(BF16))
        dscores.append((weights * (dweights - lanes(row_dot))).astype(BF16))
    return jnp.concatenate(probs, 1), jnp.concatenate(dscores, 1)


def prep_kernel(grad_ref, out_ref, log_ref, log_two_ref, row_dot_ref):
    log_two_ref[...] = log_ref[...] * LOG2E
    columns = []
    for h in range(HEADS):
        one = slice(h * HD, (h + 1) * HD)
        product = grad_ref[:, one].astype(F32) * out_ref[:, one].astype(F32)
        columns.append(jnp.sum(product, axis=1, keepdims=True))
    row_dot_ref[...] = jnp.concatenate(columns, 1).T


def remote_kernel(half_ref, query_ref, grad_ref, kv_ref, log_ref, dot_ref, part_ref, first_ref, second_ref):
    half = half_ref[0]
    rows = pl.ds(pl.multiple_of(half * SPAN, SPAN), SPAN)
    high = slice(SPAN, 2 * SPAN)
    query_high, grad_high = heads_of(query_ref, high), heads_of(grad_ref, high)
    probs, dscores = sub_block(
        kv_ref[0:SPAN, :], kv_ref[2 * SPAN : 3 * SPAN, :], query_high, grad_high, log_ref[:, high], dot_ref[:, high]
    )
    first_ref[...] = dscores
    key_low = dot(dscores, jnp.concatenate(query_high, 0), (1, 0))
    value_low = dot(probs, jnp.concatenate(grad_high, 0), (1, 0))
    query_half, grad_half = heads_of(query_ref, rows), heads_of(grad_ref, rows)
    is_low = half == 0
    probs, dscores = sub_block(
        kv_ref[rows, :],
        kv_ref[pl.ds(pl.multiple_of((half + 2) * SPAN, SPAN), SPAN), :],
        query_half,
        grad_half,
        jnp.where(is_low, log_ref[:, 0:SPAN], log_ref[:, high]),
        jnp.where(is_low, dot_ref[:, 0:SPAN], dot_ref[:, high]),
    )
    second_ref[...] = dscores
    key_half = dot(dscores, jnp.concatenate(query_half, 0), (1, 0))
    value_half = dot(probs, jnp.concatenate(grad_half, 0), (1, 0))
    part_ref[0:SPAN, :] = (key_low + jnp.where(is_low, key_half, 0.0)).astype(BF16)
    part_ref[SPAN : 2 * SPAN, :] = jnp.where(is_low, 0.0, key_half).astype(BF16)
    part_ref[2 * SPAN : 3 * SPAN, :] = (value_low + jnp.where(is_low, value_half, 0.0)).astype(BF16)
    part_ref[3 * SPAN :, :] = jnp.where(is_low, 0.0, value_half).astype(BF16)


def own_kernel(
    half_ref,
    query_ref,
    grad_ref,
    kv_ref,
    log_ref,
    dot_ref,
    kv1_ref,
    kv2_ref,
    kv3_ref,
    first1_ref,
    second1_ref,
    first2_ref,
    second2_ref,
    first3_ref,
    second3_ref,
    query_grad_ref,
    key_grad_ref,
    value_grad_ref,
):
    low, high = slice(0, SPAN), slice(SPAN, 2 * SPAN)
    span = (SPAN, 2 * SPAN)
    keys = lax.broadcasted_iota(jnp.int32, span, 0)
    mask = keys <= lax.rem(lax.broadcasted_iota(jnp.int32, span, 1), SPAN)
    query_low, grad_low = heads_of(query_ref, low), heads_of(grad_ref, low)
    query_high, grad_high = heads_of(query_ref, high), heads_of(grad_ref, high)
    key_low, key_high = kv_ref[low, :], kv_ref[high, :]
    value_low, value_high = kv_ref[2 * SPAN : 3 * SPAN, :], kv_ref[3 * SPAN :, :]
    log_low, log_high, dot_low, dot_high = log_ref[:, low], log_ref[:, high], dot_ref[:, low], dot_ref[:, high]
    probs_ll, ds_ll = sub_block(key_low, value_low, query_low, grad_low, log_low, dot_low, mask)
    probs_lh, ds_lh = sub_block(key_low, value_low, query_high, grad_high, log_high, dot_high)
    probs_hh, ds_hh = sub_block(key_high, value_high, query_high, grad_high, log_high, dot_high, mask)
    all_low, all_high = jnp.concatenate(query_low, 0), jnp.concatenate(query_high, 0)
    key_grad_ref[low, :] = dot(ds_ll, all_low, (1, 0)) + dot(ds_lh, all_high, (1, 0))
    key_grad_ref[high, :] = dot(ds_hh, all_high, (1, 0))
    all_low, all_high = jnp.concatenate(grad_low, 0), jnp.concatenate(grad_high, 0)
    value_grad_ref[low, :] = dot(probs_ll, all_low, (1, 0)) + dot(probs_lh, all_high, (1, 0))
    value_grad_ref[high, :] = dot(probs_hh, all_high, (1, 0))

    zero = jnp.zeros((SPAN, HD), BF16)
    low_keys, low_scores = [key_low], [ds_ll]
    high_keys, high_scores = [key_low, key_high], [ds_lh, ds_hh]
    remotes = ((kv1_ref, first1_ref, second1_ref), (kv2_ref, first2_ref, second2_ref), (kv3_ref, first3_ref, second3_ref))
    for j, (ref, first, second) in enumerate(remotes):
        is_low = half_ref[j] == 0
        high_keys += [ref[low, :], jnp.where(is_low, zero, ref[high, :])]
        high_scores += [first[...], second[...]]
        low_keys.append(jnp.where(is_low, ref[low, :], zero))
        low_scores.append(second[...])
    for rows, key_list, score_list in ((low, low_keys, low_scores), (high, high_keys, high_scores)):
        total = dot(jnp.concatenate(key_list, 0).T, jnp.concatenate(score_list, 0), (1, 0)) * FACTOR
        for h in range(HEADS):
            one = slice(h * HD, (h + 1) * HD)
            query_grad_ref[rows, one] = total[:, one].T.astype(BF16)


VMEM = pl.BlockSpec(memory_space=pltpu.VMEM)
SMEM = pl.BlockSpec(memory_space=pltpu.SMEM)
PARAMS = pltpu.CompilerParams(vmem_limit_bytes=24 << 20)


def units(count):
    return pl.CostEstimate(flops=count * 10 * SPAN * HD * SPAN * HEADS, bytes_accessed=1 << 20, transcendentals=count * SPAN * SPAN * HEADS)


def shifted(shard, by_outer, by_inner):
    outer, inner = lax.axis_size("outer"), lax.axis_size("inner")
    pairs = [
        (o * inner + i, (o + by_outer) % outer * inner + (i + by_inner) % inner) for o in range(outer) for i in range(inner)
    ]
    return lax.ppermute(shard, ("outer", "inner"), pairs)


def per_device(queries, key_rows, value_rows, out_grad, outputs, log_sum, span_table):
    rows = 2 * SPAN
    outer_count, inner_count = lax.axis_size("outer"), lax.axis_size("inner")
    outer_index, inner_index = lax.axis_index("outer"), lax.axis_index("inner")

    def leading(a, b):
        source = (outer_index - a) % outer_count * inner_count + (inner_index - b) % inner_count
        return span_table[source, 0]

    steps = ((1, 0), (0, 1), (1, 1))
    own = leading(0, 0)
    halves = jnp.stack([(leading(a, b) > own).astype(jnp.int32) for a, b in steps])
    packed = jnp.concatenate([key_rows, value_rows], 0)
    arrived = [shifted(packed, a, b) for a, b in steps]
    log_two, row_dot = pl.pallas_call(
        prep_kernel,
        out_shape=(pltpu.VMEM((HEADS, rows), F32), pltpu.VMEM((HEADS, rows), F32)),
        in_specs=[VMEM] * 3,
        out_specs=(VMEM, VMEM),
        compiler_params=PARAMS,
        name="row_dots",
    )(out_grad, outputs, log_sum)
    returned, scores = [], []
    for j, (a, b) in enumerate(steps):
        part, first, second = pl.pallas_call(
            remote_kernel,
            out_shape=(
                jax.ShapeDtypeStruct((2 * rows, HD), BF16),
                pltpu.VMEM((SPAN, WIDE), BF16),
                pltpu.VMEM((SPAN, WIDE), BF16),
            ),
            in_specs=[SMEM] + [VMEM] * 5,
            out_specs=(VMEM, VMEM, VMEM),
            compiler_params=PARAMS,
            cost_estimate=units(2),
            name="remote_block",
        )(halves[j : j + 1], queries, out_grad, arrived[j], log_two, row_dot)
        returned.append(shifted(part, -a, -b))
        scores += [first, second]
    query_grad, key_own, value_own = pl.pallas_call(
        own_kernel,
        out_shape=(
            jax.ShapeDtypeStruct((rows, WIDE), BF16),
            pltpu.VMEM((rows, HD), F32),
            pltpu.VMEM((rows, HD), F32),
        ),
        in_specs=[SMEM] + [VMEM] * 14,
        out_specs=(VMEM, VMEM, VMEM),
        compiler_params=PARAMS,
        cost_estimate=units(4),
        name="own_block",
    )(halves, queries, out_grad, packed, log_two, row_dot, *arrived, *scores)
    key_total = key_own
    value_total = value_own
    for part in returned:
        key_total = key_total + part[:rows].astype(F32)
        value_total = value_total + part[rows:].astype(F32)
    return (query_grad, key_total * FACTOR, value_total)


def solution(mesh):
    tokens = P(("outer", "inner"), None)
    return jax.shard_map(
        per_device,
        mesh=mesh,
        in_specs=(tokens,) * 5 + (P(None, ("outer", "inner")), P()),
        out_specs=(tokens,) * 3,
        check_vma=False,
    )
```

```python
import functools
import math

import jax
import jax.numpy as jnp
from jax import lax
from jax.experimental import pallas as pl
from jax.experimental.pallas import tpu as pltpu
from jax.sharding import PartitionSpec as P

F32 = jnp.float32
BF16 = jnp.bfloat16
HEADS = 16
HD = 128
SPAN = 128
WIDE = HEADS * HD
FACTOR = 1.0 / math.sqrt(HD)
OUTER = 16
INNER = 32
STEPS = ((1, 0), (0, 1), (1, 1))
LOG2E = math.log2(math.e)


def dot(a, b, contract):
    return lax.dot_general(a, b, ((contract[:1], contract[1:]), ((), ())), preferred_element_type=F32)


def stacked(ref, rows):
    return jnp.concatenate([ref[rows, h * HD : (h + 1) * HD] for h in range(HEADS)], 0)


def sub_block(key, value, query_ref, grad_ref, rows, log_two, row_dot, mask=None, ready=None):
    probs, dscores = [], []
    for m in range(0, HEADS, 2):
        if ready is not None:
            ready(m)
        one, two = slice(m * HD, (m + 1) * HD), slice((m + 1) * HD, (m + 2) * HD)
        pair = jnp.concatenate([query_ref[rows, one], query_ref[rows, two]], 0)
        grad = jnp.concatenate([grad_ref[rows, one], grad_ref[rows, two]], 0)
        lanes = lambda of: jnp.concatenate([of(m), of(m + 1)], 1)
        scores = dot(key, pair, (1, 1))
        weights = jnp.exp2(scores * (FACTOR * LOG2E) - lanes(log_two))
        if mask is not None:
            weights = jnp.where(mask, weights, 0.0)
        dweights = dot(value, grad, (1, 1))
        probs.append(weights.astype(BF16))
        dscores.append((weights * (dweights - lanes(row_dot))).astype(BF16))
    return jnp.concatenate(probs, 1), jnp.concatenate(dscores, 1)


def of_rows(ref, rows):
    return lambda h: ref[h : h + 1, rows]


def of_half(ref, is_low):
    return lambda h: jnp.where(is_low, ref[h : h + 1, 0:SPAN], ref[h : h + 1, SPAN:])


def pack_kernel(
    place_ref,
    table_hbm,
    key_hbm,
    value_hbm,
    query_hbm,
    grad_hbm,
    out_hbm,
    sum_hbm,
    packed_ref,
    halves_ref,
    log_ref,
    dot_ref,
    query_ref,
    grad_ref,
    out_ref,
    sum_ref,
    table_ref,
    sems,
):
    rows = 2 * SPAN
    copies = [
        pltpu.make_async_copy(table_hbm, table_ref, sems.at[2]),
        pltpu.make_async_copy(key_hbm, packed_ref.at[0:rows], sems.at[0]),
        pltpu.make_async_copy(value_hbm, packed_ref.at[rows : 2 * rows], sems.at[1]),
    ]
    for copy in copies:
        copy.start()
    pairs = ((sum_hbm, sum_ref), (grad_hbm, grad_ref), (out_hbm, out_ref), (query_hbm, query_ref))
    wide = [pltpu.make_async_copy(source, target, sems.at[i + 3]) for i, (source, target) in enumerate(pairs)]
    for copy in wide:
        copy.start()
    outer, inner = place_ref[0] // INNER, place_ref[0] % INNER
    copies[0].wait()
    own = table_ref[0, outer * INNER + inner]
    for j, (a, b) in enumerate(STEPS):
        source = (outer - a + OUTER) % OUTER * INNER + (inner - b + INNER) % INNER
        halves_ref[j] = (table_ref[0, source] > own).astype(jnp.int32)
    copies[1].wait()
    copies[2].wait()
    wide[0].wait()
    log_ref[...] = sum_ref[...] * LOG2E
    wide[1].wait()
    wide[2].wait()
    dot_ref[...] = row_dots(grad_ref, out_ref)
    wide[3].wait()


def row_dots(grad_ref, out_ref):
    columns = []
    for h in range(HEADS):
        one = slice(h * HD, (h + 1) * HD)
        product = grad_ref[:, one].astype(F32) * out_ref[:, one].astype(F32)
        columns.append(jnp.sum(product, axis=1, keepdims=True))
    return jnp.concatenate(columns, 1).T


def remote_kernel(j, half_ref, query_ref, grad_ref, kv_ref, log_ref, dot_ref, part_ref, first_ref, second_ref):
    remote_block(j, half_ref, query_ref, grad_ref, kv_ref, log_ref, dot_ref, part_ref, first_ref, second_ref)


def remote_block(j, half_ref, query_ref, grad_ref, kv_ref, log_ref, dot_ref, part_ref, first_ref, second_ref, ready=None):
    half = half_ref[j]
    rows = pl.ds(pl.multiple_of(half * SPAN, SPAN), SPAN)
    high = slice(SPAN, 2 * SPAN)
    key, value = kv_ref[0:SPAN, :], kv_ref[2 * SPAN : 3 * SPAN, :]
    probs, dscores = sub_block(
        key, value, query_ref, grad_ref, high, of_rows(log_ref, high), of_rows(dot_ref, high), ready=ready
    )
    first_ref[...] = dscores
    key_low = dot(dscores, stacked(query_ref, high), (1, 0))
    value_low = dot(probs, stacked(grad_ref, high), (1, 0))
    is_low = half == 0
    key, value = kv_ref[rows, :], kv_ref[pl.ds(pl.multiple_of((half + 2) * SPAN, SPAN), SPAN), :]
    probs, dscores = sub_block(
        key, value, query_ref, grad_ref, rows, of_half(log_ref, is_low), of_half(dot_ref, is_low)
    )
    second_ref[...] = dscores
    key_half = dot(dscores, stacked(query_ref, rows), (1, 0))
    value_half = dot(probs, stacked(grad_ref, rows), (1, 0))
    part_ref[0:SPAN, :] = (key_low + jnp.where(is_low, key_half, 0.0)).astype(BF16)
    part_ref[SPAN : 2 * SPAN, :] = jnp.where(is_low, 0.0, key_half).astype(BF16)
    part_ref[2 * SPAN : 3 * SPAN, :] = (value_low + jnp.where(is_low, value_half, 0.0)).astype(BF16)
    part_ref[3 * SPAN :, :] = jnp.where(is_low, 0.0, value_half).astype(BF16)


def own_kernel(
    half_ref,
    query_ref,
    grad_ref,
    kv_ref,
    log_ref,
    dot_ref,
    kv1_ref,
    kv2_ref,
    kv3_ref,
    first1_ref,
    second1_ref,
    first2_ref,
    second2_ref,
    first3_ref,
    second3_ref,
    query_grad_hbm,
    key_grad_ref,
    value_grad_ref,
    query_grad_ref,
    sems,
):
    low, high = slice(0, SPAN), slice(SPAN, 2 * SPAN)
    span = (SPAN, 2 * SPAN)
    keys = lax.broadcasted_iota(jnp.int32, span, 0)
    mask = keys <= lax.rem(lax.broadcasted_iota(jnp.int32, span, 1), SPAN)
    key_low, key_high = kv_ref[low, :], kv_ref[high, :]
    value_low, value_high = kv_ref[2 * SPAN : 3 * SPAN, :], kv_ref[3 * SPAN :, :]

    def block(key, value, rows, mask=None):
        probs, dscores = sub_block(
            key, value, query_ref, grad_ref, rows, of_rows(log_ref, rows), of_rows(dot_ref, rows), mask
        )
        key_part = dot(dscores, stacked(query_ref, rows), (1, 0))
        return key_part, dot(probs, stacked(grad_ref, rows), (1, 0)), dscores

    zero = jnp.zeros((SPAN, HD), BF16)
    remotes = ((kv1_ref, first1_ref, second1_ref), (kv2_ref, first2_ref, second2_ref), (kv3_ref, first3_ref, second3_ref))

    def query_part(rows, keys, scores):
        total = dot(jnp.concatenate(keys, 0).T, jnp.concatenate(scores, 0), (1, 0)) * FACTOR
        for h in range(HEADS):
            one = slice(h * HD, (h + 1) * HD)
            query_grad_ref[rows, one] = total[:, one].T.astype(BF16)
        copy = pltpu.make_async_copy(query_grad_ref.at[rows], query_grad_hbm.at[rows], sems.at[rows.start // SPAN])
        copy.start()
        return copy

    key_lh, value_lh, ds_lh = block(key_low, value_low, high)
    key_hh, value_hh, ds_hh = block(key_high, value_high, high, mask)
    keys, scores = [key_low, key_high], [ds_lh, ds_hh]
    for j, (ref, first, second) in enumerate(remotes):
        keys += [ref[low, :], jnp.where(half_ref[j] == 0, zero, ref[high, :])]
        scores += [first[...], second[...]]
    copy_high = query_part(high, keys, scores)
    key_ll, value_ll, ds_ll = block(key_low, value_low, low, mask)
    keys, scores = [key_low], [ds_ll]
    for j, (ref, first, second) in enumerate(remotes):
        keys.append(jnp.where(half_ref[j] == 0, ref[low, :], zero))
        scores.append(second[...])
    copy_low = query_part(low, keys, scores)
    key_grad_ref[low, :] = key_ll + key_lh
    key_grad_ref[high, :] = key_hh
    value_grad_ref[low, :] = value_ll + value_lh
    value_grad_ref[high, :] = value_hh
    copy_high.wait()
    copy_low.wait()


VMEM = pl.BlockSpec(memory_space=pltpu.VMEM)
ANY = pl.BlockSpec(memory_space=pl.ANY)
SMEM = pl.BlockSpec(memory_space=pltpu.SMEM)
PARAMS = pltpu.CompilerParams(vmem_limit_bytes=24 << 20)


def units(count):
    return pl.CostEstimate(flops=count * 10 * SPAN * HD * SPAN * HEADS, bytes_accessed=1 << 20, transcendentals=count * SPAN * SPAN * HEADS)


def shifted(shard, by_outer, by_inner):
    outer, inner = lax.axis_size("outer"), lax.axis_size("inner")
    pairs = [
        (o * inner + i, (o + by_outer) % outer * inner + (i + by_inner) % inner) for o in range(outer) for i in range(inner)
    ]
    return lax.ppermute(shard, ("outer", "inner"), pairs)


def per_device(queries, key_rows, value_rows, out_grad, outputs, log_sum, span_table):
    rows = 2 * SPAN
    place = lax.axis_index(("outer", "inner")).reshape(1)
    table, key_rows, value_rows, queries, out_grad, outputs, log_sum = (
        pltpu.with_memory_space_constraint(x, pltpu.HBM)
        for x in (span_table.T, key_rows, value_rows, queries, out_grad, outputs, log_sum)
    )
    packed, halves, log_two, row_dot, queries, out_grad = pl.pallas_call(
        pack_kernel,
        out_shape=(
            pltpu.VMEM((2 * rows, HD), BF16),
            pltpu.SMEM((len(STEPS),), jnp.int32),
            pltpu.VMEM((HEADS, rows), F32),
            pltpu.VMEM((HEADS, rows), F32),
            pltpu.VMEM((rows, WIDE), BF16),
            pltpu.VMEM((rows, WIDE), BF16),
        ),
        in_specs=[SMEM] + [ANY] * 7,
        out_specs=(VMEM, SMEM) + (VMEM,) * 4,
        scratch_shapes=[
            pltpu.VMEM((rows, WIDE), BF16),
            pltpu.VMEM((HEADS, rows), F32),
            pltpu.SMEM((2, OUTER * INNER), jnp.int32),
            pltpu.SemaphoreType.DMA((7,)),
        ],
        compiler_params=PARAMS,
        name="pack",
    )(place, table, key_rows, value_rows, queries, out_grad, outputs, log_sum)
    arrived = [shifted(packed, a, b) for a, b in STEPS]
    returned, scores = [], []
    for j, (a, b) in enumerate(STEPS):
        part, first, second = pl.pallas_call(
            functools.partial(remote_kernel, j),
            out_shape=(
                pltpu.VMEM((2 * rows, HD), BF16),
                pltpu.VMEM((SPAN, WIDE), BF16),
                pltpu.VMEM((SPAN, WIDE), BF16),
            ),
            in_specs=[SMEM] + [VMEM] * 5,
            out_specs=(VMEM,) * 3,
            compiler_params=PARAMS,
            cost_estimate=units(2),
            name="remote_block",
        )(halves, queries, out_grad, arrived[j], log_two, row_dot)
        returned.append(shifted(part, -a, -b))
        scores += [first, second]
    query_grad, key_own, value_own = pl.pallas_call(
        own_kernel,
        out_shape=(
            pltpu.HBM((rows, WIDE), BF16),
            pltpu.VMEM((rows, HD), F32),
            pltpu.VMEM((rows, HD), F32),
        ),
        in_specs=[SMEM] + [VMEM] * 14,
        out_specs=(ANY, VMEM, VMEM),
        scratch_shapes=[pltpu.VMEM((rows, WIDE), BF16), pltpu.SemaphoreType.DMA((2,))],
        compiler_params=PARAMS,
        cost_estimate=units(4),
        name="own_block",
    )(halves, queries, out_grad, packed, log_two, row_dot, *arrived, *scores)
    key_total = key_own
    value_total = value_own
    for part in returned:
        key_total = key_total + part[:rows].astype(F32)
        value_total = value_total + part[rows:].astype(F32)
    return (query_grad, key_total * FACTOR, value_total)


def solution(mesh):
    tokens = P(("outer", "inner"), None)
    return jax.shard_map(
        per_device,
        mesh=mesh,
        in_specs=(tokens,) * 5 + (P(None, ("outer", "inner")), P()),
        out_specs=(tokens,) * 3,
        check_vma=False,
    )
```

```python
import functools
import math

import jax
import jax.numpy as jnp
from jax import lax
from jax.experimental import pallas as pl
from jax.experimental.pallas import tpu as pltpu
from jax.sharding import PartitionSpec as P

F32 = jnp.float32
BF16 = jnp.bfloat16
HEADS = 16
HD = 128
SPAN = 128
WIDE = HEADS * HD
FACTOR = 1.0 / math.sqrt(HD)
OUTER = 16
INNER = 32
STEPS = ((1, 0), (1, 1), (0, 1))
EARLY = 4
LOG2E = math.log2(math.e)


def dot(a, b, contract):
    return lax.dot_general(a, b, ((contract[:1], contract[1:]), ((), ())), preferred_element_type=F32)


def stacked(ref, rows):
    return jnp.concatenate([ref[rows, h * HD : (h + 1) * HD] for h in range(HEADS)], 0)


def sub_block(key, value, query_ref, grad_ref, rows, log_two, row_dot, mask=None, ready=None):
    probs, dscores = [], []
    for m in range(0, HEADS, 2):
        if ready is not None:
            ready(m)
        one, two = slice(m * HD, (m + 1) * HD), slice((m + 1) * HD, (m + 2) * HD)
        pair = jnp.concatenate([query_ref[rows, one], query_ref[rows, two]], 0)
        grad = jnp.concatenate([grad_ref[rows, one], grad_ref[rows, two]], 0)
        lanes = lambda of: jnp.concatenate([of(m), of(m + 1)], 1)
        scores = dot(key, pair, (1, 1))
        weights = jnp.exp2(scores * (FACTOR * LOG2E) - lanes(log_two))
        if mask is not None:
            weights = jnp.where(mask, weights, 0.0)
        dweights = dot(value, grad, (1, 1))
        probs.append(weights.astype(BF16))
        dscores.append((weights * (dweights - lanes(row_dot))).astype(BF16))
    return jnp.concatenate(probs, 1), jnp.concatenate(dscores, 1)


def of_rows(ref, rows):
    return lambda h: ref[h : h + 1, rows]


def of_half(ref, is_low):
    return lambda h: jnp.where(is_low, ref[h : h + 1, 0:SPAN], ref[h : h + 1, SPAN:])


def pack_kernel(place_ref, table_hbm, key_hbm, value_hbm, packed_ref, plan_ref, table_ref, sems):
    rows = 2 * SPAN
    copies = [
        pltpu.make_async_copy(table_hbm, table_ref, sems.at[0]),
        pltpu.make_async_copy(key_hbm, packed_ref.at[0:rows], sems.at[1]),
        pltpu.make_async_copy(value_hbm, packed_ref.at[rows : 2 * rows], sems.at[2]),
    ]
    for copy in copies:
        copy.start()
    outer, inner = place_ref[0] // INNER, place_ref[0] % INNER
    plan_ref[len(STEPS)] = (inner < EARLY).astype(jnp.int32)
    copies[0].wait()
    own = table_ref[0, outer * INNER + inner]
    for j, (a, b) in enumerate(STEPS):
        source = (outer - a + OUTER) % OUTER * INNER + (inner - b + INNER) % INNER
        plan_ref[j] = (table_ref[0, source] > own).astype(jnp.int32)
    copies[1].wait()
    copies[2].wait()


def load_kernel(
    plan_ref,
    query_hbm,
    grad_hbm,
    out_hbm,
    sum_hbm,
    kv_ref,
    query_ref,
    grad_ref,
    log_ref,
    dot_ref,
    own_scores_ref,
    key_grad_ref,
    value_grad_ref,
    out_ref,
    sum_ref,
    sems,
):
    first = pltpu.make_async_copy(sum_hbm, sum_ref, sems.at[0])
    first.start()
    halves = (slice(0, SPAN), slice(SPAN, 2 * SPAN))
    pairs = ((grad_hbm, grad_ref), (out_hbm, out_ref), (query_hbm, query_ref))
    copies = [[pltpu.make_async_copy(a.at[r], b.at[r], sems.at[1 + 2 * i + n]) for n, r in enumerate(halves)] for i, (a, b) in enumerate(pairs)]
    for n in range(2):
        copies[0][n].start()
        copies[1][n].start()
    for n in range(2):
        copies[2][n].start()
    first.wait()
    log_ref[...] = sum_ref[...] * LOG2E
    for n, r in enumerate(halves):
        copies[0][n].wait()
        copies[1][n].wait()
        dot_ref[:, r] = row_dots(grad_ref, out_ref, r)
    for n in range(2):
        copies[2][n].wait()

    @pl.when(plan_ref[len(STEPS)] != 0)
    def _():
        own_block(query_ref, grad_ref, kv_ref, log_ref, dot_ref, own_scores_ref, key_grad_ref, value_grad_ref)


def own_block(query_ref, grad_ref, kv_ref, log_ref, dot_ref, scores_ref, key_grad_ref, value_grad_ref):
    low, high = slice(0, SPAN), slice(SPAN, 2 * SPAN)
    span = (SPAN, 2 * SPAN)
    keys = lax.broadcasted_iota(jnp.int32, span, 0)
    mask = keys <= lax.rem(lax.broadcasted_iota(jnp.int32, span, 1), SPAN)
    key_low, key_high = kv_ref[low, :], kv_ref[high, :]
    value_low, value_high = kv_ref[2 * SPAN : 3 * SPAN, :], kv_ref[3 * SPAN :, :]

    def block(n, key, value, rows, mask=None):
        probs, dscores = sub_block(
            key, value, query_ref, grad_ref, rows, of_rows(log_ref, rows), of_rows(dot_ref, rows), mask
        )
        scores_ref[n * SPAN : (n + 1) * SPAN, :] = dscores
        return dot(dscores, stacked(query_ref, rows), (1, 0)), dot(probs, stacked(grad_ref, rows), (1, 0))

    key_ll, value_ll = block(0, key_low, value_low, low, mask)
    key_lh, value_lh = block(1, key_low, value_low, high)
    key_hh, value_hh = block(2, key_high, value_high, high, mask)
    key_grad_ref[low, :] = key_ll + key_lh
    key_grad_ref[high, :] = key_hh
    value_grad_ref[low, :] = value_ll + value_lh
    value_grad_ref[high, :] = value_hh


def row_dots(grad_ref, out_ref, rows):
    columns = []
    for h in range(HEADS):
        one = slice(h * HD, (h + 1) * HD)
        product = grad_ref[rows, one].astype(F32) * out_ref[rows, one].astype(F32)
        columns.append(jnp.sum(product, axis=1, keepdims=True))
    return jnp.concatenate(columns, 1).T


def remote_low(query_ref, grad_ref, kv_refs, log_ref, dot_ref, scores_ref):
    high = slice(SPAN, 2 * SPAN)
    key = jnp.concatenate([ref[0:SPAN, :] for ref in kv_refs], 0)
    value = jnp.concatenate([ref[2 * SPAN : 3 * SPAN, :] for ref in kv_refs], 0)
    probs, dscores = sub_block(key, value, query_ref, grad_ref, high, of_rows(log_ref, high), of_rows(dot_ref, high))
    scores_ref[...] = dscores
    return dot(dscores, stacked(query_ref, high), (1, 0)), dot(probs, stacked(grad_ref, high), (1, 0))


def remote_half(half, query_ref, grad_ref, kv_ref, log_ref, dot_ref, scores_ref, key_low, value_low):
    rows = pl.ds(pl.multiple_of(half * SPAN, SPAN), SPAN)
    is_low = half == 0
    key, value = kv_ref[rows, :], kv_ref[pl.ds(pl.multiple_of((half + 2) * SPAN, SPAN), SPAN), :]
    probs, dscores = sub_block(
        key, value, query_ref, grad_ref, rows, of_half(log_ref, is_low), of_half(dot_ref, is_low)
    )
    scores_ref[...] = dscores
    key_half = dot(dscores, stacked(query_ref, rows), (1, 0))
    value_half = dot(probs, stacked(grad_ref, rows), (1, 0))
    return jnp.concatenate(
        [
            key_low + jnp.where(is_low, key_half, 0.0),
            jnp.where(is_low, 0.0, key_half),
            value_low + jnp.where(is_low, value_half, 0.0),
            jnp.where(is_low, 0.0, value_half),
        ],
        0,
    )


def outer_kernel(plan_ref, query_ref, grad_ref, kv_ref, log_ref, dot_ref, part_ref, low_ref, half_ref):
    key_low, value_low = remote_low(query_ref, grad_ref, (kv_ref,), log_ref, dot_ref, low_ref)
    part_ref[...] = remote_half(
        plan_ref[0], query_ref, grad_ref, kv_ref, log_ref, dot_ref, half_ref, key_low, value_low
    ).astype(BF16)


def inner_kernel(
    plan_ref, query_ref, grad_ref, kv1_ref, kv2_ref, log_ref, dot_ref, part1_ref, part2_ref, low_ref, half_ref
):
    key_low, value_low = remote_low(query_ref, grad_ref, (kv1_ref, kv2_ref), log_ref, dot_ref, low_ref)
    for j, (kv_ref, part_ref) in enumerate(((kv1_ref, part1_ref), (kv2_ref, part2_ref))):
        rows = slice(j * SPAN, (j + 1) * SPAN)
        part_ref[...] = remote_half(
            plan_ref[1 + j],
            query_ref,
            grad_ref,
            kv_ref,
            log_ref,
            dot_ref,
            half_ref.at[rows],
            key_low[rows],
            value_low[rows],
        ).astype(BF16)


def last_kernel(
    plan_ref,
    query_ref,
    grad_ref,
    kv_ref,
    log_ref,
    dot_ref,
    kv1_ref,
    kv2_ref,
    kv3_ref,
    low1_ref,
    half1_ref,
    low23_ref,
    half23_ref,
    _own_scores,
    _key_grad,
    _value_grad,
    query_grad_hbm,
    scores_ref,
    key_grad_ref,
    value_grad_ref,
    query_grad_ref,
    sems,
):
    @pl.when(plan_ref[len(STEPS)] == 0)
    def _():
        own_block(query_ref, grad_ref, kv_ref, log_ref, dot_ref, scores_ref, key_grad_ref, value_grad_ref)

    low, high = slice(0, SPAN), slice(SPAN, 2 * SPAN)
    zero = jnp.zeros((SPAN, HD), BF16)
    remotes = (
        (kv1_ref, low1_ref, half1_ref),
        (kv2_ref, low23_ref.at[low], half23_ref.at[low]),
        (kv3_ref, low23_ref.at[high], half23_ref.at[high]),
    )

    def query_part(n, rows, keys, scores):
        total = dot(jnp.concatenate(keys, 0).T, jnp.concatenate(scores, 0), (1, 0)) * FACTOR
        for h in range(HEADS):
            one = slice(h * HD, (h + 1) * HD)
            query_grad_ref[rows, one] = total[:, one].T.astype(BF16)
        copy = pltpu.make_async_copy(query_grad_ref.at[rows], query_grad_hbm.at[rows], sems.at[n])
        copy.start()
        return copy

    keys, scores = [kv_ref[low, :], kv_ref[high, :]], [scores_ref[SPAN : 2 * SPAN, :], scores_ref[2 * SPAN :, :]]
    for j, (ref, first, second) in enumerate(remotes):
        keys += [ref[low, :], jnp.where(plan_ref[j] == 0, zero, ref[high, :])]
        scores += [first[...], second[...]]
    copy_high = query_part(1, high, keys, scores)
    keys, scores = [kv_ref[low, :]], [scores_ref[low, :]]
    for j, (ref, first, second) in enumerate(remotes):
        keys.append(jnp.where(plan_ref[j] == 0, ref[low, :], zero))
        scores.append(second[...])
    copy_low = query_part(0, low, keys, scores)
    copy_high.wait()
    copy_low.wait()


VMEM = pl.BlockSpec(memory_space=pltpu.VMEM)
ANY = pl.BlockSpec(memory_space=pl.ANY)
SMEM = pl.BlockSpec(memory_space=pltpu.SMEM)
PARAMS = pltpu.CompilerParams(vmem_limit_bytes=24 << 20)


def units(count):
    return pl.CostEstimate(flops=count * 10 * SPAN * HD * SPAN * HEADS, bytes_accessed=1 << 20, transcendentals=count * SPAN * SPAN * HEADS)


def shifted(shard, by_outer, by_inner):
    outer, inner = lax.axis_size("outer"), lax.axis_size("inner")
    pairs = [
        (o * inner + i, (o + by_outer) % outer * inner + (i + by_inner) % inner) for o in range(outer) for i in range(inner)
    ]
    return lax.ppermute(shard, ("outer", "inner"), pairs)


def per_device(queries, key_rows, value_rows, out_grad, outputs, log_sum, span_table):
    rows = 2 * SPAN
    place = lax.axis_index(("outer", "inner")).reshape(1)
    table, key_rows, value_rows, queries, out_grad, outputs, log_sum = (
        pltpu.with_memory_space_constraint(x, pltpu.HBM)
        for x in (span_table.T, key_rows, value_rows, queries, out_grad, outputs, log_sum)
    )
    packed, plan = pl.pallas_call(
        pack_kernel,
        out_shape=(pltpu.VMEM((2 * rows, HD), BF16), pltpu.SMEM((len(STEPS) + 1,), jnp.int32)),
        in_specs=[SMEM] + [ANY] * 3,
        out_specs=(VMEM, SMEM),
        scratch_shapes=[pltpu.SMEM((2, OUTER * INNER), jnp.int32), pltpu.SemaphoreType.DMA((3,))],
        compiler_params=PARAMS,
        name="pack",
    )(place, table, key_rows, value_rows)
    arrived = [shifted(packed, a, b) for a, b in STEPS]
    wide = pltpu.VMEM((rows, WIDE), BF16)
    small = pltpu.VMEM((HEADS, rows), F32)
    part = pltpu.VMEM((2 * rows, HD), BF16)
    total = pltpu.VMEM((rows, HD), F32)

    def spans(count):
        return pltpu.VMEM((count * SPAN, WIDE), BF16)

    queries, out_grad, log_two, row_dot, own_scores, key_own, value_own = pl.pallas_call(
        load_kernel,
        out_shape=(wide, wide, small, small, spans(3), total, total),
        in_specs=[SMEM] + [ANY] * 4 + [VMEM],
        out_specs=(VMEM,) * 7,
        scratch_shapes=[wide, small, pltpu.SemaphoreType.DMA((7,))],
        compiler_params=PARAMS,
        cost_estimate=units(2),
        name="load",
    )(plan, queries, out_grad, outputs, log_sum, packed)
    part1, low1, half1 = pl.pallas_call(
        outer_kernel,
        out_shape=(part, spans(1), spans(1)),
        in_specs=[SMEM] + [VMEM] * 5,
        out_specs=(VMEM,) * 3,
        compiler_params=PARAMS,
        cost_estimate=units(2),
        name="outer_block",
    )(plan, queries, out_grad, arrived[0], log_two, row_dot)
    back = [shifted(part1, -1, 0)]
    part2, part3, low23, half23 = pl.pallas_call(
        inner_kernel,
        out_shape=(part, part, spans(2), spans(2)),
        in_specs=[SMEM] + [VMEM] * 6,
        out_specs=(VMEM,) * 4,
        compiler_params=PARAMS,
        cost_estimate=units(4),
        name="inner_blocks",
    )(plan, queries, out_grad, arrived[1], arrived[2], log_two, row_dot)
    back += [shifted(part2, -1, -1), shifted(part3, 0, -1)]
    query_grad, _, key_total, value_total = pl.pallas_call(
        last_kernel,
        out_shape=(pltpu.HBM((rows, WIDE), BF16), spans(3), total, total),
        in_specs=[SMEM] + [VMEM] * 15,
        out_specs=(ANY, VMEM, VMEM, VMEM),
        scratch_shapes=[wide, pltpu.SemaphoreType.DMA((2,))],
        input_output_aliases={13: 1, 14: 2, 15: 3},
        compiler_params=PARAMS,
        cost_estimate=units(4),
        name="last",
    )(
        plan,
        queries,
        out_grad,
        packed,
        log_two,
        row_dot,
        *arrived,
        low1,
        half1,
        low23,
        half23,
        own_scores,
        key_own,
        value_own,
    )
    for one in back:
        key_total = key_total + one[:rows].astype(F32)
        value_total = value_total + one[rows:].astype(F32)
    return (query_grad, key_total * FACTOR, value_total)


def solution(mesh):
    tokens = P(("outer", "inner"), None)
    return jax.shard_map(
        per_device,
        mesh=mesh,
        in_specs=(tokens,) * 5 + (P(None, ("outer", "inner")), P()),
        out_specs=(tokens,) * 3,
        check_vma=False,
    )
```

```python
import functools
import math

import jax
import jax.numpy as jnp
from jax import lax
from jax.experimental import pallas as pl
from jax.experimental.pallas import tpu as pltpu
from jax.sharding import PartitionSpec as P

F32 = jnp.float32
BF16 = jnp.bfloat16
HEADS = 16
HD = 128
SPAN = 128
WIDE = HEADS * HD
FACTOR = 1.0 / math.sqrt(HD)
OUTER = 16
INNER = 32
STEPS = ((1, 0), (0, 1), (1, 1))
EARLY = 4
LOG2E = math.log2(math.e)


def dot(a, b, contract):
    return lax.dot_general(a, b, ((contract[:1], contract[1:]), ((), ())), preferred_element_type=F32)


def stacked(ref, rows):
    return jnp.concatenate([ref[rows, h * HD : (h + 1) * HD] for h in range(HEADS)], 0)


def sub_block(key, value, query_ref, grad_ref, rows, log_two, row_dot, mask=None, ready=None):
    probs, dscores = [], []
    for m in range(0, HEADS, 2):
        if ready is not None:
            ready(m)
        one, two = slice(m * HD, (m + 1) * HD), slice((m + 1) * HD, (m + 2) * HD)
        pair = jnp.concatenate([query_ref[rows, one], query_ref[rows, two]], 0)
        grad = jnp.concatenate([grad_ref[rows, one], grad_ref[rows, two]], 0)
        lanes = lambda of: jnp.concatenate([of(m), of(m + 1)], 1)
        scores = dot(key, pair, (1, 1))
        weights = jnp.exp2(scores * (FACTOR * LOG2E) - lanes(log_two))
        if mask is not None:
            weights = jnp.where(mask, weights, 0.0)
        dweights = dot(value, grad, (1, 1))
        probs.append(weights.astype(BF16))
        dscores.append((weights * (dweights - lanes(row_dot))).astype(BF16))
    return jnp.concatenate(probs, 1), jnp.concatenate(dscores, 1)


def of_rows(ref, rows):
    return lambda h: ref[h : h + 1, rows]


def of_half(ref, is_low):
    return lambda h: jnp.where(is_low, ref[h : h + 1, 0:SPAN], ref[h : h + 1, SPAN:])


def pack_kernel(place_ref, table_hbm, key_hbm, value_hbm, packed_ref, plan_ref, table_ref, sems):
    rows = 2 * SPAN
    copies = [
        pltpu.make_async_copy(table_hbm, table_ref, sems.at[0]),
        pltpu.make_async_copy(key_hbm, packed_ref.at[0:rows], sems.at[1]),
        pltpu.make_async_copy(value_hbm, packed_ref.at[rows : 2 * rows], sems.at[2]),
    ]
    for copy in copies:
        copy.start()
    outer, inner = place_ref[0] // INNER, place_ref[0] % INNER
    plan_ref[len(STEPS)] = (inner < EARLY).astype(jnp.int32)
    copies[0].wait()
    own = table_ref[0, outer * INNER + inner]
    for j, (a, b) in enumerate(STEPS):
        source = (outer - a + OUTER) % OUTER * INNER + (inner - b + INNER) % INNER
        plan_ref[j] = (table_ref[0, source] > own).astype(jnp.int32)
    copies[1].wait()
    copies[2].wait()


def load_kernel(
    plan_ref, query_ref, grad_ref, out_ref, sum_ref, kv_ref, log_ref, dot_ref, own_scores_ref, key_grad_ref, value_grad_ref
):
    log_ref[...] = sum_ref[...] * LOG2E
    dot_ref[...] = row_dots(grad_ref, out_ref, slice(0, 2 * SPAN))

    @pl.when(plan_ref[len(STEPS)] != 0)
    def _():
        own_block(query_ref, grad_ref, kv_ref, log_ref, dot_ref, own_scores_ref, key_grad_ref, value_grad_ref)


def own_block(query_ref, grad_ref, kv_ref, log_ref, dot_ref, scores_ref, key_grad_ref, value_grad_ref):
    low, high = slice(0, SPAN), slice(SPAN, 2 * SPAN)
    span = (SPAN, 2 * SPAN)
    keys = lax.broadcasted_iota(jnp.int32, span, 0)
    mask = keys <= lax.rem(lax.broadcasted_iota(jnp.int32, span, 1), SPAN)
    key_low, key_high = kv_ref[low, :], kv_ref[high, :]
    value_low, value_high = kv_ref[2 * SPAN : 3 * SPAN, :], kv_ref[3 * SPAN :, :]

    def block(n, key, value, rows, mask=None):
        probs, dscores = sub_block(
            key, value, query_ref, grad_ref, rows, of_rows(log_ref, rows), of_rows(dot_ref, rows), mask
        )
        scores_ref[n * SPAN : (n + 1) * SPAN, :] = dscores
        return dot(dscores, stacked(query_ref, rows), (1, 0)), dot(probs, stacked(grad_ref, rows), (1, 0))

    key_ll, value_ll = block(0, key_low, value_low, low, mask)
    key_lh, value_lh = block(1, key_low, value_low, high)
    key_hh, value_hh = block(2, key_high, value_high, high, mask)
    key_grad_ref[low, :] = key_ll + key_lh
    key_grad_ref[high, :] = key_hh
    value_grad_ref[low, :] = value_ll + value_lh
    value_grad_ref[high, :] = value_hh


def row_dots(grad_ref, out_ref, rows):
    columns = []
    for h in range(HEADS):
        one = slice(h * HD, (h + 1) * HD)
        product = grad_ref[rows, one].astype(F32) * out_ref[rows, one].astype(F32)
        columns.append(jnp.sum(product, axis=1, keepdims=True))
    return jnp.concatenate(columns, 1).T


def remote_low(query_ref, grad_ref, kv_ref, log_ref, dot_ref, scores_ref):
    high = slice(SPAN, 2 * SPAN)
    key, value = kv_ref[0:SPAN, :], kv_ref[2 * SPAN : 3 * SPAN, :]
    probs, dscores = sub_block(key, value, query_ref, grad_ref, high, of_rows(log_ref, high), of_rows(dot_ref, high))
    scores_ref[...] = dscores
    return dot(dscores, stacked(query_ref, high), (1, 0)), dot(probs, stacked(grad_ref, high), (1, 0))


def remote_half(half, query_ref, grad_ref, kv_ref, log_ref, dot_ref, scores_ref, key_low, value_low):
    rows = pl.ds(pl.multiple_of(half * SPAN, SPAN), SPAN)
    is_low = half == 0
    key, value = kv_ref[rows, :], kv_ref[pl.ds(pl.multiple_of((half + 2) * SPAN, SPAN), SPAN), :]
    probs, dscores = sub_block(
        key, value, query_ref, grad_ref, rows, of_half(log_ref, is_low), of_half(dot_ref, is_low)
    )
    scores_ref[...] = dscores
    key_half = dot(dscores, stacked(query_ref, rows), (1, 0))
    value_half = dot(probs, stacked(grad_ref, rows), (1, 0))
    return jnp.concatenate(
        [
            key_low + jnp.where(is_low, key_half, 0.0),
            jnp.where(is_low, 0.0, key_half),
            value_low + jnp.where(is_low, value_half, 0.0),
            jnp.where(is_low, 0.0, value_half),
        ],
        0,
    )


def remote_kernel(j, plan_ref, query_ref, grad_ref, kv_ref, log_ref, dot_ref, _before, part_ref, low_ref, half_ref):
    key_low, value_low = remote_low(query_ref, grad_ref, kv_ref, log_ref, dot_ref, low_ref)
    part_ref[...] = remote_half(
        plan_ref[j], query_ref, grad_ref, kv_ref, log_ref, dot_ref, half_ref, key_low, value_low
    ).astype(BF16)


def last_kernel(
    plan_ref,
    query_ref,
    grad_ref,
    kv_ref,
    log_ref,
    dot_ref,
    kv1_ref,
    kv2_ref,
    kv3_ref,
    low1_ref,
    half1_ref,
    low2_ref,
    half2_ref,
    low3_ref,
    half3_ref,
    _own_scores,
    _key_grad,
    _value_grad,
    query_grad_hbm,
    scores_ref,
    key_grad_ref,
    value_grad_ref,
    query_grad_ref,
    sems,
):
    @pl.when(plan_ref[len(STEPS)] == 0)
    def _():
        own_block(query_ref, grad_ref, kv_ref, log_ref, dot_ref, scores_ref, key_grad_ref, value_grad_ref)

    low, high = slice(0, SPAN), slice(SPAN, 2 * SPAN)
    zero = jnp.zeros((SPAN, HD), BF16)
    remotes = (
        (kv1_ref, low1_ref, half1_ref),
        (kv2_ref, low2_ref, half2_ref),
        (kv3_ref, low3_ref, half3_ref),
    )

    def query_part(n, rows, keys, scores):
        total = dot(jnp.concatenate(keys, 0).T, jnp.concatenate(scores, 0), (1, 0)) * FACTOR
        for h in range(HEADS):
            one = slice(h * HD, (h + 1) * HD)
            query_grad_ref[rows, one] = total[:, one].T.astype(BF16)
        copy = pltpu.make_async_copy(query_grad_ref.at[rows], query_grad_hbm.at[rows], sems.at[n])
        copy.start()
        return copy

    keys, scores = [kv_ref[low, :], kv_ref[high, :]], [scores_ref[SPAN : 2 * SPAN, :], scores_ref[2 * SPAN :, :]]
    for j, (ref, first, second) in enumerate(remotes):
        keys += [ref[low, :], jnp.where(plan_ref[j] == 0, zero, ref[high, :])]
        scores += [first[...], second[...]]
    copy_high = query_part(1, high, keys, scores)
    keys, scores = [kv_ref[low, :]], [scores_ref[low, :]]
    for j, (ref, first, second) in enumerate(remotes):
        keys.append(jnp.where(plan_ref[j] == 0, ref[low, :], zero))
        scores.append(second[...])
    copy_low = query_part(0, low, keys, scores)
    copy_high.wait()
    copy_low.wait()


VMEM = pl.BlockSpec(memory_space=pltpu.VMEM)
ANY = pl.BlockSpec(memory_space=pl.ANY)
SMEM = pl.BlockSpec(memory_space=pltpu.SMEM)
PARAMS = pltpu.CompilerParams(vmem_limit_bytes=24 << 20)


def units(count):
    return pl.CostEstimate(flops=count * 10 * SPAN * HD * SPAN * HEADS, bytes_accessed=1 << 20, transcendentals=count * SPAN * SPAN * HEADS)


def shifted(shard, by_outer, by_inner):
    outer, inner = lax.axis_size("outer"), lax.axis_size("inner")
    pairs = [
        (o * inner + i, (o + by_outer) % outer * inner + (i + by_inner) % inner) for o in range(outer) for i in range(inner)
    ]
    return lax.ppermute(shard, ("outer", "inner"), pairs)


def per_device(queries, key_rows, value_rows, out_grad, outputs, log_sum, span_table):
    rows = 2 * SPAN
    place = lax.axis_index(("outer", "inner")).reshape(1)
    table, key_rows, value_rows = (
        pltpu.with_memory_space_constraint(x, pltpu.HBM)
        for x in (span_table.T, key_rows, value_rows)
    )
    packed, plan = pl.pallas_call(
        pack_kernel,
        out_shape=(pltpu.VMEM((2 * rows, HD), BF16), pltpu.SMEM((len(STEPS) + 1,), jnp.int32)),
        in_specs=[SMEM] + [ANY] * 3,
        out_specs=(VMEM, SMEM),
        scratch_shapes=[pltpu.SMEM((2, OUTER * INNER), jnp.int32), pltpu.SemaphoreType.DMA((3,))],
        compiler_params=PARAMS,
        cost_estimate=pl.CostEstimate(flops=10**10, bytes_accessed=0, transcendentals=0),
        name="pack",
    )(place, table, key_rows, value_rows)
    arrived = [shifted(packed, a, b) for a, b in STEPS]
    wide = pltpu.VMEM((rows, WIDE), BF16)
    small = pltpu.VMEM((HEADS, rows), F32)
    part = pltpu.VMEM((2 * rows, HD), BF16)
    total = pltpu.VMEM((rows, HD), F32)

    def spans(count):
        return pltpu.VMEM((count * SPAN, WIDE), BF16)

    log_two, row_dot, own_scores, key_own, value_own = pl.pallas_call(
        load_kernel,
        out_shape=(small, small, spans(3), total, total),
        in_specs=[SMEM] + [VMEM] * 5,
        out_specs=(VMEM,) * 5,
        compiler_params=PARAMS,
        cost_estimate=units(2),
        name="load",
    )(plan, queries, out_grad, outputs, log_sum, packed)
    back, scores = [], []
    half = row_dot
    for j, (a, b) in enumerate(STEPS):
        one, low, half = pl.pallas_call(
            functools.partial(remote_kernel, j),
            out_shape=(part, spans(1), spans(1)),
            in_specs=[SMEM] + [VMEM] * 5 + [ANY],
            out_specs=(VMEM,) * 3,
            compiler_params=PARAMS,
            cost_estimate=units(2),
            name="remote_block",
        )(plan, queries, out_grad, arrived[j], log_two, row_dot, half)
        back.append(shifted(one, -a, -b))
        scores += [low, half]
    query_grad, _, key_total, value_total = pl.pallas_call(
        last_kernel,
        out_shape=(pltpu.HBM((rows, WIDE), BF16), spans(3), total, total),
        in_specs=[SMEM] + [VMEM] * 17,
        out_specs=(ANY, VMEM, VMEM, VMEM),
        scratch_shapes=[wide, pltpu.SemaphoreType.DMA((2,))],
        input_output_aliases={15: 1, 16: 2, 17: 3},
        compiler_params=PARAMS,
        cost_estimate=units(4),
        name="last",
    )(
        plan,
        queries,
        out_grad,
        packed,
        log_two,
        row_dot,
        *arrived,
        *scores,
        own_scores,
        key_own,
        value_own,
    )
    for one in back:
        key_total = key_total + one[:rows].astype(F32)
        value_total = value_total + one[rows:].astype(F32)
    return (query_grad, key_total * FACTOR, value_total)


def solution(mesh):
    tokens = P(("outer", "inner"), None)
    return jax.shard_map(
        per_device,
        mesh=mesh,
        in_specs=(tokens,) * 5 + (P(None, ("outer", "inner")), P()),
        out_specs=(tokens,) * 3,
        check_vma=False,
    )
```

```python
import functools
import math

import jax
import jax.numpy as jnp
from jax import lax
from jax.experimental import pallas as pl
from jax.experimental.pallas import tpu as pltpu
from jax.sharding import PartitionSpec as P

F32 = jnp.float32
BF16 = jnp.bfloat16
HEADS = 16
HD = 128
SPAN = 128
WIDE = HEADS * HD
FACTOR = 1.0 / math.sqrt(HD)
OUTER = 16
INNER = 32
STEPS = ((1, 0), (0, 1), (1, 1))
EARLY = 4
LOG2E = math.log2(math.e)


def dot(a, b, contract):
    return lax.dot_general(a, b, ((contract[:1], contract[1:]), ((), ())), preferred_element_type=F32)


def stacked(ref, rows):
    return jnp.concatenate([ref[rows, h * HD : (h + 1) * HD] for h in range(HEADS)], 0)


def sub_block(key, value, query_ref, grad_ref, rows, log_two, row_dot, mask=None, ready=None):
    probs, dscores = [], []
    for m in range(0, HEADS, 2):
        if ready is not None:
            ready(m)
        one, two = slice(m * HD, (m + 1) * HD), slice((m + 1) * HD, (m + 2) * HD)
        pair = jnp.concatenate([query_ref[rows, one], query_ref[rows, two]], 0)
        grad = jnp.concatenate([grad_ref[rows, one], grad_ref[rows, two]], 0)
        lanes = lambda of: jnp.concatenate([of(m), of(m + 1)], 1)
        scores = dot(key, pair, (1, 1))
        weights = jnp.exp2(scores * (FACTOR * LOG2E) - lanes(log_two))
        if mask is not None:
            weights = jnp.where(mask, weights, 0.0)
        dweights = dot(value, grad, (1, 1))
        probs.append(weights.astype(BF16))
        dscores.append((weights * (dweights - lanes(row_dot))).astype(BF16))
    return jnp.concatenate(probs, 1), jnp.concatenate(dscores, 1)


def of_rows(ref, rows):
    return lambda h: ref[h : h + 1, rows]


def of_half(ref, is_low):
    return lambda h: jnp.where(is_low, ref[h : h + 1, 0:SPAN], ref[h : h + 1, SPAN:])


def pack_kernel(place_ref, table_hbm, key_hbm, value_hbm, packed_ref, plan_ref, table_ref, sems):
    rows = 2 * SPAN
    copies = [
        pltpu.make_async_copy(table_hbm, table_ref, sems.at[0]),
        pltpu.make_async_copy(key_hbm, packed_ref.at[0:rows], sems.at[1]),
        pltpu.make_async_copy(value_hbm, packed_ref.at[rows : 2 * rows], sems.at[2]),
    ]
    for n in (1, 2, 0):
        copies[n].start()
    outer, inner = place_ref[0] // INNER, place_ref[0] % INNER
    plan_ref[len(STEPS)] = (inner < EARLY).astype(jnp.int32)
    copies[0].wait()
    own = table_ref[0, outer * INNER + inner]
    for j, (a, b) in enumerate(STEPS):
        source = (outer - a + OUTER) % OUTER * INNER + (inner - b + INNER) % INNER
        plan_ref[j] = (table_ref[0, source] > own).astype(jnp.int32)
    copies[1].wait()
    copies[2].wait()


def load_kernel(
    plan_ref, query_ref, grad_ref, out_ref, sum_ref, kv_ref, log_ref, dot_ref, own_scores_ref, key_grad_ref, value_grad_ref
):
    log_ref[...] = sum_ref[...] * LOG2E
    dot_ref[...] = row_dots(grad_ref, out_ref, slice(0, 2 * SPAN))

    @pl.when(plan_ref[len(STEPS)] != 0)
    def _():
        own_block(query_ref, grad_ref, kv_ref, log_ref, dot_ref, own_scores_ref, key_grad_ref, value_grad_ref)


def own_block(query_ref, grad_ref, kv_ref, log_ref, dot_ref, scores_ref, key_grad_ref, value_grad_ref):
    low, high = slice(0, SPAN), slice(SPAN, 2 * SPAN)
    span = (SPAN, 2 * SPAN)
    keys = lax.broadcasted_iota(jnp.int32, span, 0)
    mask = keys <= lax.rem(lax.broadcasted_iota(jnp.int32, span, 1), SPAN)
    key_low, key_high = kv_ref[low, :], kv_ref[high, :]
    value_low, value_high = kv_ref[2 * SPAN : 3 * SPAN, :], kv_ref[3 * SPAN :, :]

    def block(n, key, value, rows, mask=None):
        probs, dscores = sub_block(
            key, value, query_ref, grad_ref, rows, of_rows(log_ref, rows), of_rows(dot_ref, rows), mask
        )
        scores_ref[n * SPAN : (n + 1) * SPAN, :] = dscores
        return dot(dscores, stacked(query_ref, rows), (1, 0)), dot(probs, stacked(grad_ref, rows), (1, 0))

    key_ll, value_ll = block(0, key_low, value_low, low, mask)
    key_lh, value_lh = block(1, key_low, value_low, high)
    key_hh, value_hh = block(2, key_high, value_high, high, mask)
    key_grad_ref[low, :] = key_ll + key_lh
    key_grad_ref[high, :] = key_hh
    value_grad_ref[low, :] = value_ll + value_lh
    value_grad_ref[high, :] = value_hh


def row_dots(grad_ref, out_ref, rows):
    columns = []
    for h in range(HEADS):
        one = slice(h * HD, (h + 1) * HD)
        product = grad_ref[rows, one].astype(F32) * out_ref[rows, one].astype(F32)
        columns.append(jnp.sum(product, axis=1, keepdims=True))
    return jnp.concatenate(columns, 1).T


def remote_low(query_ref, grad_ref, kv_ref, log_ref, dot_ref, scores_ref):
    high = slice(SPAN, 2 * SPAN)
    key, value = kv_ref[0:SPAN, :], kv_ref[2 * SPAN : 3 * SPAN, :]
    probs, dscores = sub_block(key, value, query_ref, grad_ref, high, of_rows(log_ref, high), of_rows(dot_ref, high))
    scores_ref[...] = dscores
    return dot(dscores, stacked(query_ref, high), (1, 0)), dot(probs, stacked(grad_ref, high), (1, 0))


def remote_half(half, query_ref, grad_ref, kv_ref, log_ref, dot_ref, scores_ref, key_low, value_low):
    rows = pl.ds(pl.multiple_of(half * SPAN, SPAN), SPAN)
    is_low = half == 0
    key, value = kv_ref[rows, :], kv_ref[pl.ds(pl.multiple_of((half + 2) * SPAN, SPAN), SPAN), :]
    probs, dscores = sub_block(
        key, value, query_ref, grad_ref, rows, of_half(log_ref, is_low), of_half(dot_ref, is_low)
    )
    scores_ref[...] = dscores
    key_half = dot(dscores, stacked(query_ref, rows), (1, 0))
    value_half = dot(probs, stacked(grad_ref, rows), (1, 0))
    return jnp.concatenate(
        [
            key_low + jnp.where(is_low, key_half, 0.0),
            jnp.where(is_low, 0.0, key_half),
            value_low + jnp.where(is_low, value_half, 0.0),
            jnp.where(is_low, 0.0, value_half),
        ],
        0,
    )


def remote_kernel(j, plan_ref, query_ref, grad_ref, kv_ref, log_ref, dot_ref, _before, part_ref, low_ref, half_ref):
    key_low, value_low = remote_low(query_ref, grad_ref, kv_ref, log_ref, dot_ref, low_ref)
    part_ref[...] = remote_half(
        plan_ref[j], query_ref, grad_ref, kv_ref, log_ref, dot_ref, half_ref, key_low, value_low
    ).astype(BF16)


def last_kernel(
    plan_ref,
    query_ref,
    grad_ref,
    kv_ref,
    log_ref,
    dot_ref,
    kv1_ref,
    kv2_ref,
    kv3_ref,
    low1_ref,
    half1_ref,
    low2_ref,
    half2_ref,
    low3_ref,
    half3_ref,
    _own_scores,
    _key_grad,
    _value_grad,
    query_grad_hbm,
    scores_ref,
    key_grad_ref,
    value_grad_ref,
    query_grad_ref,
    sems,
):
    @pl.when(plan_ref[len(STEPS)] == 0)
    def _():
        own_block(query_ref, grad_ref, kv_ref, log_ref, dot_ref, scores_ref, key_grad_ref, value_grad_ref)

    low, high = slice(0, SPAN), slice(SPAN, 2 * SPAN)
    zero = jnp.zeros((SPAN, HD), BF16)
    remotes = (
        (kv1_ref, low1_ref, half1_ref),
        (kv2_ref, low2_ref, half2_ref),
        (kv3_ref, low3_ref, half3_ref),
    )

    def query_part(n, rows, keys, scores):
        total = dot(jnp.concatenate(keys, 0).T, jnp.concatenate(scores, 0), (1, 0)) * FACTOR
        for h in range(HEADS):
            one = slice(h * HD, (h + 1) * HD)
            query_grad_ref[rows, one] = total[:, one].T.astype(BF16)
        copy = pltpu.make_async_copy(query_grad_ref.at[rows], query_grad_hbm.at[rows], sems.at[n])
        copy.start()
        return copy

    keys, scores = [kv_ref[low, :], kv_ref[high, :]], [scores_ref[SPAN : 2 * SPAN, :], scores_ref[2 * SPAN :, :]]
    for j, (ref, first, second) in enumerate(remotes):
        keys += [ref[low, :], jnp.where(plan_ref[j] == 0, zero, ref[high, :])]
        scores += [first[...], second[...]]
    copy_high = query_part(1, high, keys, scores)
    keys, scores = [kv_ref[low, :]], [scores_ref[low, :]]
    for j, (ref, first, second) in enumerate(remotes):
        keys.append(jnp.where(plan_ref[j] == 0, ref[low, :], zero))
        scores.append(second[...])
    copy_low = query_part(0, low, keys, scores)
    copy_high.wait()
    copy_low.wait()


def total_kernel(key_ref, value_ref, one_ref, two_ref, three_ref, key_hbm, value_hbm, key_sum_ref, value_sum_ref, sems):
    rows = 2 * SPAN
    copies = []
    for n, (own, target, out, factor) in enumerate(
        ((key_ref, key_sum_ref, key_hbm, FACTOR), (value_ref, value_sum_ref, value_hbm, None))
    ):
        part = slice(n * rows, (n + 1) * rows)
        total = own[...]
        for ref in (one_ref, two_ref, three_ref):
            total = total + ref[part, :].astype(F32)
        target[...] = total if factor is None else total * factor
        copies.append(pltpu.make_async_copy(target, out, sems.at[n]))
        copies[n].start()
    for copy in copies:
        copy.wait()


VMEM = pl.BlockSpec(memory_space=pltpu.VMEM)
ANY = pl.BlockSpec(memory_space=pl.ANY)
SMEM = pl.BlockSpec(memory_space=pltpu.SMEM)
PARAMS = pltpu.CompilerParams(vmem_limit_bytes=24 << 20)


def units(count):
    return pl.CostEstimate(flops=count * 10 * SPAN * HD * SPAN * HEADS, bytes_accessed=1 << 20, transcendentals=count * SPAN * SPAN * HEADS)


def shifted(shard, by_outer, by_inner):
    outer, inner = lax.axis_size("outer"), lax.axis_size("inner")
    pairs = [
        (o * inner + i, (o + by_outer) % outer * inner + (i + by_inner) % inner) for o in range(outer) for i in range(inner)
    ]
    return lax.ppermute(shard, ("outer", "inner"), pairs)


def per_device(queries, key_rows, value_rows, out_grad, outputs, log_sum, span_table):
    rows = 2 * SPAN
    place = lax.axis_index(("outer", "inner")).reshape(1)
    table, key_rows, value_rows = (
        pltpu.with_memory_space_constraint(x, pltpu.HBM)
        for x in (span_table.T, key_rows, value_rows)
    )
    packed, plan = pl.pallas_call(
        pack_kernel,
        out_shape=(pltpu.VMEM((2 * rows, HD), BF16), pltpu.SMEM((len(STEPS) + 1,), jnp.int32)),
        in_specs=[SMEM] + [ANY] * 3,
        out_specs=(VMEM, SMEM),
        scratch_shapes=[pltpu.SMEM((2, OUTER * INNER), jnp.int32), pltpu.SemaphoreType.DMA((3,))],
        compiler_params=PARAMS,
        cost_estimate=pl.CostEstimate(flops=10**10, bytes_accessed=0, transcendentals=0),
        name="pack",
    )(place, table, key_rows, value_rows)
    arrived = [shifted(packed, a, b) for a, b in STEPS]
    wide = pltpu.VMEM((rows, WIDE), BF16)
    small = pltpu.VMEM((HEADS, rows), F32)
    part = pltpu.VMEM((2 * rows, HD), BF16)
    total = pltpu.VMEM((rows, HD), F32)

    def spans(count):
        return pltpu.VMEM((count * SPAN, WIDE), BF16)

    log_two, row_dot, own_scores, key_own, value_own = pl.pallas_call(
        load_kernel,
        out_shape=(small, small, spans(3), total, total),
        in_specs=[SMEM] + [VMEM] * 5,
        out_specs=(VMEM,) * 5,
        compiler_params=PARAMS,
        cost_estimate=units(2),
        name="load",
    )(plan, queries, out_grad, outputs, log_sum, packed)
    back, scores = [], []
    half = row_dot
    for j, (a, b) in enumerate(STEPS):
        one, low, half = pl.pallas_call(
            functools.partial(remote_kernel, j),
            out_shape=(part, spans(1), spans(1)),
            in_specs=[SMEM] + [VMEM] * 5 + [ANY],
            out_specs=(VMEM,) * 3,
            compiler_params=PARAMS,
            cost_estimate=units(2),
            name="remote_block",
        )(plan, queries, out_grad, arrived[j], log_two, row_dot, half)
        back.append(shifted(one, -a, -b))
        scores += [low, half]
    query_grad, _, key_total, value_total = pl.pallas_call(
        last_kernel,
        out_shape=(pltpu.HBM((rows, WIDE), BF16), spans(3), total, total),
        in_specs=[SMEM] + [VMEM] * 17,
        out_specs=(ANY, VMEM, VMEM, VMEM),
        scratch_shapes=[wide, pltpu.SemaphoreType.DMA((2,))],
        input_output_aliases={15: 1, 16: 2, 17: 3},
        compiler_params=PARAMS,
        cost_estimate=units(4),
        name="last",
    )(
        plan,
        queries,
        out_grad,
        packed,
        log_two,
        row_dot,
        *arrived,
        *scores,
        own_scores,
        key_own,
        value_own,
    )
    key_total, value_total = pl.pallas_call(
        total_kernel,
        out_shape=(pltpu.HBM((rows, HD), F32), pltpu.HBM((rows, HD), F32)),
        in_specs=[VMEM] * 5,
        out_specs=(ANY, ANY),
        scratch_shapes=[total, total, pltpu.SemaphoreType.DMA((2,))],
        compiler_params=PARAMS,
        name="totals",
    )(key_total, value_total, *back)
    return (query_grad, key_total, value_total)


def solution(mesh):
    tokens = P(("outer", "inner"), None)
    return jax.shard_map(
        per_device,
        mesh=mesh,
        in_specs=(tokens,) * 5 + (P(None, ("outer", "inner")), P()),
        out_specs=(tokens,) * 3,
        check_vma=False,
    )
```

```python
import functools
import math

import jax
import jax.numpy as jnp
from jax import lax
from jax.experimental import pallas as pl
from jax.experimental.pallas import tpu as pltpu
from jax.sharding import PartitionSpec as P

F32 = jnp.float32
BF16 = jnp.bfloat16
HEADS = 16
HD = 128
SPAN = 128
WIDE = HEADS * HD
FACTOR = 1.0 / math.sqrt(HD)
OUTER = 16
INNER = 32
STEPS = ((1, 0), (0, 1), (1, 1))
EARLY = 2
LOG2E = math.log2(math.e)


def dot(a, b, contract):
    return lax.dot_general(a, b, ((contract[:1], contract[1:]), ((), ())), preferred_element_type=F32)


def stacked(ref, rows):
    return jnp.concatenate([ref[rows, h * HD : (h + 1) * HD] for h in range(HEADS)], 0)


def sub_block(key, value, query_ref, grad_ref, rows, log_two, row_dot, mask=None, ready=None):
    probs, dscores = [], []
    for m in range(0, HEADS, 2):
        if ready is not None:
            ready(m)
        one, two = slice(m * HD, (m + 1) * HD), slice((m + 1) * HD, (m + 2) * HD)
        pair = jnp.concatenate([query_ref[rows, one], query_ref[rows, two]], 0)
        grad = jnp.concatenate([grad_ref[rows, one], grad_ref[rows, two]], 0)
        lanes = lambda of: jnp.concatenate([of(m), of(m + 1)], 1)
        scores = dot(key, pair, (1, 1))
        weights = jnp.exp2(scores * (FACTOR * LOG2E) - lanes(log_two))
        if mask is not None:
            weights = jnp.where(mask, weights, 0.0)
        dweights = dot(value, grad, (1, 1))
        probs.append(weights.astype(BF16))
        dscores.append((weights * (dweights - lanes(row_dot))).astype(BF16))
    return jnp.concatenate(probs, 1), jnp.concatenate(dscores, 1)


def of_rows(ref, rows):
    return lambda h: ref[h : h + 1, rows]


def of_half(ref, is_low):
    return lambda h: jnp.where(is_low, ref[h : h + 1, 0:SPAN], ref[h : h + 1, SPAN:])


def pack_kernel(place_ref, table_hbm, key_hbm, value_hbm, packed_ref, plan_ref, table_ref, sems):
    rows = 2 * SPAN
    copies = [
        pltpu.make_async_copy(table_hbm, table_ref, sems.at[0]),
        pltpu.make_async_copy(key_hbm, packed_ref.at[0:rows], sems.at[1]),
        pltpu.make_async_copy(value_hbm, packed_ref.at[rows : 2 * rows], sems.at[2]),
    ]
    for copy in copies:
        copy.start()
    outer, inner = place_ref[0] // INNER, place_ref[0] % INNER
    plan_ref[len(STEPS)] = (inner < EARLY).astype(jnp.int32)
    copies[0].wait()
    own = table_ref[0, outer * INNER + inner]
    for j, (a, b) in enumerate(STEPS):
        source = (outer - a + OUTER) % OUTER * INNER + (inner - b + INNER) % INNER
        plan_ref[j] = (table_ref[0, source] > own).astype(jnp.int32)
    copies[1].wait()
    copies[2].wait()


def load_kernel(
    plan_ref, query_ref, grad_ref, out_ref, sum_ref, kv_ref, log_ref, dot_ref, own_scores_ref, key_grad_ref, value_grad_ref
):
    log_ref[...] = sum_ref[...] * LOG2E
    dot_ref[...] = row_dots(grad_ref, out_ref, slice(0, 2 * SPAN))

    @pl.when(plan_ref[len(STEPS)] != 0)
    def _():
        own_block(query_ref, grad_ref, kv_ref, log_ref, dot_ref, own_scores_ref, key_grad_ref, value_grad_ref)


def own_block(query_ref, grad_ref, kv_ref, log_ref, dot_ref, scores_ref, key_grad_ref, value_grad_ref):
    low, high = slice(0, SPAN), slice(SPAN, 2 * SPAN)
    span = (SPAN, 2 * SPAN)
    keys = lax.broadcasted_iota(jnp.int32, span, 0)
    mask = keys <= lax.rem(lax.broadcasted_iota(jnp.int32, span, 1), SPAN)
    key_low, key_high = kv_ref[low, :], kv_ref[high, :]
    value_low, value_high = kv_ref[2 * SPAN : 3 * SPAN, :], kv_ref[3 * SPAN :, :]

    def block(n, key, value, rows, mask=None):
        probs, dscores = sub_block(
            key, value, query_ref, grad_ref, rows, of_rows(log_ref, rows), of_rows(dot_ref, rows), mask
        )
        scores_ref[n * SPAN : (n + 1) * SPAN, :] = dscores
        return dot(dscores, stacked(query_ref, rows), (1, 0)), dot(probs, stacked(grad_ref, rows), (1, 0))

    key_ll, value_ll = block(0, key_low, value_low, low, mask)
    key_lh, value_lh = block(1, key_low, value_low, high)
    key_hh, value_hh = block(2, key_high, value_high, high, mask)
    key_grad_ref[low, :] = key_ll + key_lh
    key_grad_ref[high, :] = key_hh
    value_grad_ref[low, :] = value_ll + value_lh
    value_grad_ref[high, :] = value_hh


def row_dots(grad_ref, out_ref, rows):
    columns = []
    for h in range(HEADS):
        one = slice(h * HD, (h + 1) * HD)
        product = grad_ref[rows, one].astype(F32) * out_ref[rows, one].astype(F32)
        columns.append(jnp.sum(product, axis=1, keepdims=True))
    return jnp.concatenate(columns, 1).T


def remote_low(query_ref, grad_ref, kv_ref, log_ref, dot_ref, scores_ref):
    high = slice(SPAN, 2 * SPAN)
    key, value = kv_ref[0:SPAN, :], kv_ref[2 * SPAN : 3 * SPAN, :]
    probs, dscores = sub_block(key, value, query_ref, grad_ref, high, of_rows(log_ref, high), of_rows(dot_ref, high))
    scores_ref[...] = dscores
    return dot(dscores, stacked(query_ref, high), (1, 0)), dot(probs, stacked(grad_ref, high), (1, 0))


def remote_half(half, query_ref, grad_ref, kv_ref, log_ref, dot_ref, scores_ref, key_low, value_low):
    rows = pl.ds(pl.multiple_of(half * SPAN, SPAN), SPAN)
    is_low = half == 0
    key, value = kv_ref[rows, :], kv_ref[pl.ds(pl.multiple_of((half + 2) * SPAN, SPAN), SPAN), :]
    probs, dscores = sub_block(
        key, value, query_ref, grad_ref, rows, of_half(log_ref, is_low), of_half(dot_ref, is_low)
    )
    scores_ref[...] = dscores
    key_half = dot(dscores, stacked(query_ref, rows), (1, 0))
    value_half = dot(probs, stacked(grad_ref, rows), (1, 0))
    return jnp.concatenate(
        [
            key_low + jnp.where(is_low, key_half, 0.0),
            jnp.where(is_low, 0.0, key_half),
            value_low + jnp.where(is_low, value_half, 0.0),
            jnp.where(is_low, 0.0, value_half),
        ],
        0,
    )


def remote_kernel(j, plan_ref, query_ref, grad_ref, kv_ref, log_ref, dot_ref, _before, part_ref, low_ref, half_ref):
    key_low, value_low = remote_low(query_ref, grad_ref, kv_ref, log_ref, dot_ref, low_ref)
    part_ref[...] = remote_half(
        plan_ref[j], query_ref, grad_ref, kv_ref, log_ref, dot_ref, half_ref, key_low, value_low
    ).astype(BF16)


def last_kernel(
    plan_ref,
    query_ref,
    grad_ref,
    kv_ref,
    log_ref,
    dot_ref,
    kv1_ref,
    kv2_ref,
    kv3_ref,
    low1_ref,
    half1_ref,
    low2_ref,
    half2_ref,
    low3_ref,
    half3_ref,
    _own_scores,
    _key_grad,
    _value_grad,
    query_grad_hbm,
    scores_ref,
    key_grad_ref,
    value_grad_ref,
    query_grad_ref,
    sems,
):
    @pl.when(plan_ref[len(STEPS)] == 0)
    def _():
        own_block(query_ref, grad_ref, kv_ref, log_ref, dot_ref, scores_ref, key_grad_ref, value_grad_ref)

    low, high = slice(0, SPAN), slice(SPAN, 2 * SPAN)
    zero = jnp.zeros((SPAN, HD), BF16)
    remotes = (
        (kv1_ref, low1_ref, half1_ref),
        (kv2_ref, low2_ref, half2_ref),
        (kv3_ref, low3_ref, half3_ref),
    )

    def query_part(n, rows, keys, scores):
        total = dot(jnp.concatenate(keys, 0).T, jnp.concatenate(scores, 0), (1, 0)) * FACTOR
        for h in range(HEADS):
            one = slice(h * HD, (h + 1) * HD)
            query_grad_ref[rows, one] = total[:, one].T.astype(BF16)
        copy = pltpu.make_async_copy(query_grad_ref.at[rows], query_grad_hbm.at[rows], sems.at[n])
        copy.start()
        return copy

    keys, scores = [kv_ref[low, :], kv_ref[high, :]], [scores_ref[SPAN : 2 * SPAN, :], scores_ref[2 * SPAN :, :]]
    for j, (ref, first, second) in enumerate(remotes):
        keys += [ref[low, :], jnp.where(plan_ref[j] == 0, zero, ref[high, :])]
        scores += [first[...], second[...]]
    copy_high = query_part(1, high, keys, scores)
    keys, scores = [kv_ref[low, :]], [scores_ref[low, :]]
    for j, (ref, first, second) in enumerate(remotes):
        keys.append(jnp.where(plan_ref[j] == 0, ref[low, :], zero))
        scores.append(second[...])
    copy_low = query_part(0, low, keys, scores)
    copy_high.wait()
    copy_low.wait()


VMEM = pl.BlockSpec(memory_space=pltpu.VMEM)
ANY = pl.BlockSpec(memory_space=pl.ANY)
SMEM = pl.BlockSpec(memory_space=pltpu.SMEM)
PARAMS = pltpu.CompilerParams(vmem_limit_bytes=24 << 20)


def units(count):
    return pl.CostEstimate(flops=count * 10 * SPAN * HD * SPAN * HEADS, bytes_accessed=1 << 20, transcendentals=count * SPAN * SPAN * HEADS)


def shifted(shard, by_outer, by_inner):
    outer, inner = lax.axis_size("outer"), lax.axis_size("inner")
    pairs = [
        (o * inner + i, (o + by_outer) % outer * inner + (i + by_inner) % inner) for o in range(outer) for i in range(inner)
    ]
    return lax.ppermute(shard, ("outer", "inner"), pairs)


def per_device(queries, key_rows, value_rows, out_grad, outputs, log_sum, span_table):
    rows = 2 * SPAN
    place = lax.axis_index(("outer", "inner")).reshape(1)
    table, key_rows, value_rows = (
        pltpu.with_memory_space_constraint(x, pltpu.HBM)
        for x in (span_table.T, key_rows, value_rows)
    )
    packed, plan = pl.pallas_call(
        pack_kernel,
        out_shape=(pltpu.VMEM((2 * rows, HD), BF16), pltpu.SMEM((len(STEPS) + 1,), jnp.int32)),
        in_specs=[SMEM] + [ANY] * 3,
        out_specs=(VMEM, SMEM),
        scratch_shapes=[pltpu.SMEM((2, OUTER * INNER), jnp.int32), pltpu.SemaphoreType.DMA((3,))],
        compiler_params=PARAMS,
        cost_estimate=pl.CostEstimate(flops=10**10, bytes_accessed=0, transcendentals=0),
        name="pack",
    )(place, table, key_rows, value_rows)
    arrived = [shifted(packed, a, b) for a, b in STEPS]
    wide = pltpu.VMEM((rows, WIDE), BF16)
    small = pltpu.VMEM((HEADS, rows), F32)
    part = pltpu.VMEM((2 * rows, HD), BF16)
    total = pltpu.VMEM((rows, HD), F32)

    def spans(count):
        return pltpu.VMEM((count * SPAN, WIDE), BF16)

    log_two, row_dot, own_scores, key_own, value_own = pl.pallas_call(
        load_kernel,
        out_shape=(small, small, spans(3), total, total),
        in_specs=[SMEM] + [VMEM] * 5,
        out_specs=(VMEM,) * 5,
        compiler_params=PARAMS,
        cost_estimate=units(2),
        name="load",
    )(plan, queries, out_grad, outputs, log_sum, packed)
    back, scores = [], []
    half = row_dot
    for j, (a, b) in enumerate(STEPS):
        one, low, half = pl.pallas_call(
            functools.partial(remote_kernel, j),
            out_shape=(part, spans(1), spans(1)),
            in_specs=[SMEM] + [VMEM] * 5 + [ANY],
            out_specs=(VMEM,) * 3,
            compiler_params=PARAMS,
            cost_estimate=units(2),
            name="remote_block",
        )(plan, queries, out_grad, arrived[j], log_two, row_dot, half)
        back.append(shifted(one, -a, -b))
        scores += [low, half]
    query_grad, _, key_total, value_total = pl.pallas_call(
        last_kernel,
        out_shape=(pltpu.HBM((rows, WIDE), BF16), spans(3), total, total),
        in_specs=[SMEM] + [VMEM] * 17,
        out_specs=(ANY, VMEM, VMEM, VMEM),
        scratch_shapes=[wide, pltpu.SemaphoreType.DMA((2,))],
        input_output_aliases={15: 1, 16: 2, 17: 3},
        compiler_params=PARAMS,
        cost_estimate=units(4),
        name="last",
    )(
        plan,
        queries,
        out_grad,
        packed,
        log_two,
        row_dot,
        *arrived,
        *scores,
        own_scores,
        key_own,
        value_own,
    )
    for one in back:
        key_total = key_total + one[:rows].astype(F32)
        value_total = value_total + one[rows:].astype(F32)
    return (query_grad, key_total * FACTOR, value_total)


def solution(mesh):
    tokens = P(("outer", "inner"), None)
    return jax.shard_map(
        per_device,
        mesh=mesh,
        in_specs=(tokens,) * 5 + (P(None, ("outer", "inner")), P()),
        out_specs=(tokens,) * 3,
        check_vma=False,
    )
```
